32 devices in a mesh: fsdp: 32 (over z, y, x, core).
Axes of the slice: x: 2, y: 2, z: 4, core: 2. Of those that a mesh axis runs over, the one named last changes fastest.
Arguments:
- tokens: bfloat16 [8192, 1024], P('fsdp'), may hold values from -6 to 6
- w_query: bfloat16 [1024, 2048], P('fsdp'), may hold values from -0.1875 to 0.1875
- w_key: bfloat16 [1024, 1024], P('fsdp'), may hold values from -0.1875 to 0.1875
- w_value: bfloat16 [1024, 1024], P('fsdp'), may hold values from -0.1875 to 0.1875
- w_output: bfloat16 [2048, 1024], P(None, 'fsdp'), may hold values from -1 to 1
- w_gate: bfloat16 [1024, 3072], P('fsdp'), may hold values from -0.1875 to 0.1875
- w_up: bfloat16 [1024, 3072], P('fsdp'), may hold values from -0.1875 to 0.1875
- w_down: bfloat16 [3072, 1024], P(None, 'fsdp'), may hold values from -0.109375 to 0.109375
- norm_gains: bfloat16 [2304], P('fsdp'), may hold values from 0.099609375 to 1.8984375
- seq_lens: int32 [32, 4], P('fsdp'), may hold values from 0 to 256, as said below
- cotangent: bfloat16 [8192, 1024], P('fsdp'), may hold values from -6 to 6
Outputs:
- out: bfloat16 [8192, 1024], P('fsdp')
- grad_tokens: float32 [8192, 1024], P('fsdp')
- grad_query: float32 [1024, 2048], P('fsdp')
- grad_key: float32 [1024, 1024], P('fsdp')
- grad_value: float32 [1024, 1024], P('fsdp')
- grad_output: float32 [2048, 1024], P(None, 'fsdp')
- grad_gate: float32 [1024, 3072], P('fsdp')
- grad_up: float32 [1024, 3072], P('fsdp')
- grad_down: float32 [3072, 1024], P(None, 'fsdp')
- grad_gains: float32 [2304], P('fsdp')
The draws below stay inside these ranges and needn't reach their ends.
Inputs may be any that keep to these rules, and one draw needn't show every extreme that they name: `seq_lens`: row r lists the lengths of the sequences of device r; each row sums to 64 to 256; a length 0 marks an unused slot; in every draw one row is a single sequence of 256 tokens.
All inputs are finite; a program needn't handle non-finite values.
Results may differ from the reference program's by a relative error of at most 0.012.
The reference program's roundings to bfloat16 on the way count: a program that leaves them out, or rounds other values in their place, can miss the bound.
Values may be sent and summed in bfloat16 or wider, within the bound.
A program may use at most 256 MiB of HBM per device.

```python
import jax
import jax.numpy as jnp
from jax import lax

D = 1024
QUERY_HEADS = 16
VALUE_HEADS = 8
HEAD_WIDTH = 128
FF = 3072
CAP = 256
SLOTS = 4
QW = 2048
KW = 1024
GAINS = 2304
TOKENS = 8192
N_FSDP = 32


def draw_seq_lens(key, part):
    key = jax.random.fold_in(key, 7)
    key_totals, key_shares, key_full = jax.random.split(key, 3)
    totals = jax.random.randint(key_totals, (N_FSDP,), CAP // 4, CAP + 1)
    shares = jax.random.randint(key_shares, (N_FSDP, SLOTS), 1, 9)
    full_row = jax.random.randint(key_full, (), 0, N_FSDP)
    row_ids = jnp.arange(N_FSDP)
    is_full = row_ids == full_row
    totals = jnp.where(is_full, CAP, totals)
    single = (jnp.arange(SLOTS) == 0).astype(jnp.int32)
    shares = jnp.where(is_full[:, None], single[None, :], shares)
    running = jnp.cumsum(shares, axis=1)
    bounds = totals[:, None] * running // running[:, -1:]
    previous = jnp.concatenate([jnp.zeros((N_FSDP, 1), jnp.int32), bounds[:, :-1]], axis=1)
    return (bounds - previous).astype(jnp.int32)


def with_spikes(values, own_key, source, target, blocks, factor):
    def block_of(dim):
        return (jnp.arange(values.shape[dim]) // (values.shape[dim] // blocks)).reshape((-1,) + (1,) * (values.ndim - 1 - dim))

    first = jax.random.permutation(own_key, blocks)[block_of(target)]
    far = (block_of(target) + blocks // 2) % blocks
    return jnp.where((block_of(source) == first) | (block_of(source) == far), factor * values, values)


def level_of(rng, shape, pieces, least, top_value):
    gain, own = 1.0, jax.random.fold_in(rng, 6)
    for dim, blocks in pieces:
        steps = jnp.exp(jax.random.uniform(jax.random.fold_in(own, dim), (blocks,), jnp.float32, least / len(pieces), top_value / len(pieces)))
        gain = gain * jnp.repeat(steps, shape[dim] // blocks).reshape([-1 if axis == dim else 1 for axis in range(len(shape))])
    return gain


def gaussian(key, dims, scale, most, cuts=(), kind=jnp.bfloat16):
    level = level_of(key, dims, cuts, -0.22, 0.18) if cuts else 1.0
    drawn = jax.random.normal(key, dims, jnp.float32) * scale * level
    return jnp.minimum(jnp.maximum(drawn, -most), most).astype(kind)


def bell_draw_with(key, shape, scale, reach, pieces, heavy, kind=jnp.bfloat16):
    entries = scale * jax.random.normal(key, shape, jnp.float32)
    if pieces:
        entries = entries * level_of(key, shape, pieces, -0.22, 0.18)
    return jnp.clip(with_spikes(entries, jax.random.fold_in(key, 3), *heavy), -reach, reach).astype(kind)


def setup_inputs(seed: int = 0) -> dict:
    key_list = jax.random.split(jax.random.key(seed), 12)
    return {
        "tokens": gaussian(key_list[0], (TOKENS, D), 1.0, 6.0, ((0, 32),)),
        "w_query": gaussian(key_list[1], (D, QW), D ** -0.5, 0.1875, ((0, 32),)),
        "w_key": gaussian(key_list[2], (D, KW), D ** -0.5, 0.1875, ((0, 32),)),
        "w_value": gaussian(key_list[3], (D, KW), D ** -0.5, 0.1875, ((0, 32),)),
        "w_output": gaussian(key_list[4], (QW, D), (QW // 64) ** -0.5, 1.0, ((1, 32),)),
        "w_gate": gaussian(key_list[5], (D, FF), D ** -0.5, 0.1875, ((0, 32),)),
        "w_up": gaussian(key_list[6], (D, FF), D ** -0.5, 0.1875, ((0, 32),)),
        "w_down": gaussian(key_list[7], (FF, D), FF ** -0.5, 0.109375, ((1, 32),)),
        "norm_gains": jnp.clip(1.0 + 0.18 * jax.random.normal(key_list[8], (GAINS,), jnp.float32), 0.099609375, 1.8984375).astype(jnp.bfloat16),
        "seq_lens": draw_seq_lens(jax.random.fold_in(key_list[11], 71), 0),
        "cotangent": bell_draw_with(key_list[10], (TOKENS, D), 1.0, 6.0, ((0, 32),), (0, 1, 32, 2.75)),
    }


EPSILON = 1e-06
ROPE_BASE = 1000000.0
HIGHEST_PREC = lax.Precision.HIGHEST

@jax.custom_vjp
def low(v):
    return lax.optimization_barrier(v.astype(jnp.bfloat16)).astype(jnp.float32)

@jax.custom_vjp
def low_back(v):
    return v

def low_keep(v):
    return (low(v), None)

def low_pass(kept, grad):
    return (grad,)

def back_keep(v):
    return (v, None)

def back_low(kept, grad):
    return (low(grad),)
low.defvjp(low_keep, low_pass)
low_back.defvjp(back_keep, back_low)

def arrange(lengths):
    seq_ends = jnp.cumsum(lengths).astype(jnp.int32)
    seq_starts = (seq_ends - lengths).astype(jnp.int32)
    places = jnp.arange(CAP, dtype=jnp.int32)
    segment = lax.optimization_barrier(jnp.sum((places[:, None] >= seq_ends[None, :]).astype(jnp.int32), axis=1)).astype(jnp.int32)
    owned_by = segment[:, None] == jnp.arange(SLOTS, dtype=jnp.int32)[None, :]
    first_place = lax.optimization_barrier(jnp.sum(jnp.where(owned_by, seq_starts[None, :], 0), axis=1)).astype(jnp.int32)
    return (segment, (places - first_place).astype(jnp.int32))

def rope_tables(position):
    half_width = HEAD_WIDTH // 2
    inverse = ROPE_BASE ** (-(jnp.arange(half_width, dtype=jnp.float32) * 2.0 / HEAD_WIDTH))
    angles = position.astype(jnp.float32)[:, None] * inverse[None, :]
    angles = jnp.concatenate([angles, angles], axis=-1)
    return (jnp.cos(angles)[:, None, :], jnp.sin(angles)[:, None, :])

def apply_rotary(values, cosine_lookup, sine_lookup):
    half_width = values.shape[-1] // 2
    turned = jnp.concatenate([-values[..., half_width:], values[..., :half_width]], axis=-1)
    return values * cosine_lookup + turned * sine_lookup

def rescaled_rows(values):
    return values * lax.rsqrt(lax.optimization_barrier(jnp.mean(values * values, axis=-1, keepdims=True)) + EPSILON)

def matrix_product(left, right):
    return jnp.dot(left, right, precision=HIGHEST_PREC, preferred_element_type=jnp.float32)

def layer_forward(stream, query_w, key_matrix, value_matrix, out_w, gate_w, up_w, down_w, gain_all, segment, position):
    token_budget = stream.shape[0]
    query_group_width = QUERY_HEADS // VALUE_HEADS
    attn_gain = gain_all[:D]
    ffn_gain = gain_all[D:2 * D]
    query_norm_weight = gain_all[2 * D:2 * D + HEAD_WIDTH]
    key_gain = gain_all[2 * D + HEAD_WIDTH:]
    live_rows = (segment < SLOTS).astype(jnp.float32)[:, None]
    cosine_lookup, sine_lookup = rope_tables(position)
    rescaled_input = low(rescaled_rows(stream) * attn_gain)
    query_unrotated = low_back(matrix_product(rescaled_input, query_w)).reshape(token_budget, QUERY_HEADS, HEAD_WIDTH)
    key_unrotated = low_back(matrix_product(rescaled_input, key_matrix)).reshape(token_budget, VALUE_HEADS, HEAD_WIDTH)
    value_unprojected = low_back(matrix_product(rescaled_input, value_matrix)).reshape(token_budget, VALUE_HEADS, HEAD_WIDTH)
    query_rotated = low(apply_rotary(rescaled_rows(query_unrotated) * query_norm_weight, cosine_lookup, sine_lookup)).reshape(token_budget, VALUE_HEADS, query_group_width, HEAD_WIDTH)
    key_rot = low(apply_rotary(rescaled_rows(key_unrotated) * key_gain, cosine_lookup, sine_lookup))
    value_reduced = low(value_unprojected)
    raw = low_back(jnp.einsum('qkgd,lkd->kgql', query_rotated, key_rot, precision=HIGHEST_PREC))
    places = jnp.arange(token_budget, dtype=jnp.int32)
    allowed = (segment[:, None] == segment[None, :]) & (places[:, None] >= places[None, :])
    scores = jnp.where(allowed[None, None], raw * HEAD_WIDTH ** (-0.5), -1e+30)
    row_top = lax.optimization_barrier(jnp.max(scores, axis=-1, keepdims=True))
    lifted = jnp.exp(scores - row_top)
    probs = low(lifted / lax.optimization_barrier(jnp.sum(lifted, axis=-1, keepdims=True)))
    mixed = jnp.einsum('kgql,lkd->qkgd', probs, value_reduced, precision=HIGHEST_PREC).reshape(token_budget, QUERY_HEADS * HEAD_WIDTH)
    attended = low(low_back(mixed))
    branch = low_back(matrix_product(attended, out_w))
    middle = stream + live_rows * branch
    normed_mid = low(rescaled_rows(middle) * ffn_gain)
    gate_pre = low_back(matrix_product(normed_mid, gate_w))
    up_pre = low_back(matrix_product(normed_mid, up_w))
    hidden = low(gate_pre * jax.nn.sigmoid(gate_pre) * up_pre)
    return middle + live_rows * matrix_product(hidden, down_w)

def reference(tokens, w_query, w_key, w_value, w_output, w_gate, w_up, w_down, norm_gains, seq_lens, cotangent):
    weights = (w_query.astype(jnp.float32), w_key.astype(jnp.float32), w_value.astype(jnp.float32), w_output.astype(jnp.float32), w_gate.astype(jnp.float32), w_up.astype(jnp.float32), w_down.astype(jnp.float32), norm_gains.astype(jnp.float32))
    token_blocks = tokens.astype(jnp.float32).reshape(N_FSDP, CAP, D)
    cot_blocks = cotangent.astype(jnp.float32).reshape(N_FSDP, CAP, D)

    def device_step(running, device_item):
        token_block, cot_block, lengths = device_item
        segment, position = arrange(lengths)

        def run_layer(stream, *params):
            return layer_forward(stream, *params, segment, position)
        result, pullback = jax.vjp(run_layer, token_block, *weights)
        gradients = pullback(cot_block)
        running = tuple((total + part_grad for total, part_grad in zip(running, gradients[1:])))
        return (running, (result.astype(jnp.bfloat16), gradients[0]))
    initial = tuple((jnp.zeros(weight.shape, jnp.float32) for weight in weights))
    summed, (out_blocks, back_blocks) = lax.scan(device_step, initial, (token_blocks, cot_blocks, seq_lens))
    return (out_blocks.reshape(TOKENS, D), back_blocks.reshape(TOKENS, D), summed[0], summed[1], summed[2], summed[3], summed[4], summed[5], summed[6], summed[7])
```

```python
import functools

import jax
import jax.numpy as jnp
from jax import lax
from jax.sharding import PartitionSpec as P

QUERY_HEADS = 16
VALUE_HEADS = 8
HEAD_WIDTH = 128
SLOTS = 4


EPSILON = 1e-06
ROPE_BASE = 1000000.0
MASKED_SCORE = -1e30


def arrange(lengths, token_budget):
    seq_ends = jnp.cumsum(lengths)
    seq_starts = seq_ends - lengths
    places = jnp.arange(token_budget, dtype=jnp.int32)
    segment = jnp.sum((places[:, None] >= seq_ends[None, :]).astype(jnp.int32), axis=1)
    owned_by = segment[:, None] == jnp.arange(SLOTS, dtype=jnp.int32)[None, :]
    first_place = jnp.sum(jnp.where(owned_by, seq_starts[None, :], 0), axis=1)
    return (segment, places - first_place)


def rope_tables(position):
    half_width = HEAD_WIDTH // 2
    inverse = ROPE_BASE ** (-(jnp.arange(half_width, dtype=jnp.float32) * 2.0 / HEAD_WIDTH))
    angles = position.astype(jnp.float32)[:, None] * inverse[None, :]
    angles = jnp.concatenate([angles, angles], axis=-1)
    return (jnp.cos(angles)[:, None, :], jnp.sin(angles)[:, None, :])


def apply_rotary(values, cosine_lookup, sine_lookup):
    half_width = values.shape[-1] // 2
    turned = jnp.concatenate([-values[..., half_width:], values[..., :half_width]], axis=-1)
    return values * cosine_lookup + turned * sine_lookup


def rotate_back(grads, cosine_lookup, sine_lookup):
    half_width = grads.shape[-1] // 2
    turned = grads * sine_lookup
    return grads * cosine_lookup + jnp.concatenate(
        [turned[..., half_width:], -turned[..., :half_width]], axis=-1
    )


def normalize(values):
    row_scale = lax.rsqrt(jnp.mean(values * values, axis=-1, keepdims=True) + EPSILON)
    return (values * row_scale, row_scale)


def norm_back(grads, unit_vals, row_scale):
    return row_scale * (grads - unit_vals * jnp.mean(grads * unit_vals, axis=-1, keepdims=True))


def apply_projection(left, weight):
    return jnp.dot(left, weight, preferred_element_type=jnp.float32)


def back_project(grads, weight):
    return jnp.einsum("tj,ij->ti", grads, weight, preferred_element_type=jnp.float32)


def contract(left, right):
    return jnp.einsum("ti,tj->ij", left, right, preferred_element_type=jnp.float32)


def split_gains(gain_all, model_width):
    gain_all = gain_all.astype(jnp.float32)
    return (
        gain_all[:model_width],
        gain_all[model_width : 2 * model_width],
        gain_all[2 * model_width : 2 * model_width + HEAD_WIDTH],
        gain_all[2 * model_width + HEAD_WIDTH :],
    )


def block_scores(query_block, key_block, seg_rows, seg_keys, first_row):
    row_count = query_block.shape[0]
    key_count = key_block.shape[0]
    raw = jnp.einsum("qkgd,lkd->kgql", query_block, key_block, preferred_element_type=jnp.float32)
    row_at = first_row + jnp.arange(row_count, dtype=jnp.int32)
    key_at = jnp.arange(key_count, dtype=jnp.int32)
    allowed = (seg_rows[:, None] == seg_keys[None, :]) & (row_at[:, None] >= key_at[None, :])
    return jnp.where(allowed[None, None], raw * HEAD_WIDTH ** (-0.5), MASKED_SCORE)


def part_orders(device_count):
    bits = device_count.bit_length() - 1
    if bits == 5:
        return [[1, 2, 3, 4], [2, 1, 3, 4], [3, 1, 2, 4]]
    chip = list(range(1, bits))
    third = (bits - 1) // 3
    return [chip, chip[third:] + chip[:third], chip[2 * third :] + chip[: 2 * third]]


def partners(device_count, bit):
    return [(i, i ^ (1 << bit)) for i in range(device_count)]


def pick_core(me, device_count, rows, core):
    model = device_count * rows
    source = jnp.arange(model, dtype=jnp.int32)[:, None]
    target = jnp.arange(model // 2, dtype=jnp.int32)[None, :]
    wanted = ((target // rows) * 2 + core) * rows + target % rows
    return (source == wanted).astype(jnp.bfloat16)


def pick_order(me, device_count, rows, order):
    half = device_count * rows // 2
    source = jnp.arange(half, dtype=jnp.int32)[:, None]
    target = jnp.arange(half, dtype=jnp.int32)[None, :]
    far = target // rows
    chip = jnp.zeros_like(far)
    last = len(order) - 1
    for place, bit in enumerate(order):
        chip = chip + (((far >> (last - place)) & 1) << (bit - 1))
    wanted = (chip ^ (me // 2)) * rows + target % rows
    return (source == wanted).astype(jnp.bfloat16)


def exact(left, onehot):
    return jnp.dot(left, onehot, preferred_element_type=jnp.float32).astype(jnp.bfloat16)


def swap(values, device_count, bit):
    return lax.ppermute(values, "fsdp", partners(device_count, bit))


def sum_to_owner(left, right, device_count, order):
    half = left.shape[1] // 2
    sent = contract(left[:, half:], right).astype(jnp.bfloat16)
    arrived = swap(sent, device_count, order[0])
    total = contract(left[:, :half], right) + arrived.astype(jnp.float32)
    for bit in order[1:]:
        half //= 2
        arrived = swap(total[half:].astype(jnp.bfloat16), device_count, bit)
        total = total[:half] + arrived.astype(jnp.float32)
    return total


def local(
    device_count,
    tokens, w_query, w_key, w_value, w_output, w_gate, w_up, w_down, norm_gains, seq_lens, cotangent
):
    me = lax.axis_index("fsdp")
    core = me % 2
    orders = part_orders(device_count)
    token_budget = tokens.shape[0]
    model_width = tokens.shape[1]
    rows = w_query.shape[0]
    qw = w_query.shape[1]
    kw = w_key.shape[1]
    ff = w_gate.shape[1]
    own_gains = norm_gains.shape[0]
    gain_block = jnp.pad(norm_gains[None, :], ((0, rows - 1), (0, 128 - own_gains)))
    gathered = lax.all_gather(
        jnp.concatenate(
            [w_query, w_key, w_value, w_output.T, w_gate, w_up, w_down.T, gain_block], axis=1
        ),
        "fsdp",
        axis=0,
        tiled=True,
    )
    at = qw + 2 * kw
    qkv_w = gathered[:, :at]
    out_wt = gathered[:, at : at + qw]
    at = at + qw
    gate_up_w = gathered[:, at : at + 2 * ff]
    at = at + 2 * ff
    down_wt = gathered[:, at : at + ff]
    at = at + ff
    gain_all = gathered[:, at:].reshape(device_count, rows, 128)[:, 0, :own_gains].reshape(-1)

    query_group_width = QUERY_HEADS // VALUE_HEADS
    rows_per_block = token_budget
    attn_gain, ffn_gain, query_norm_weight, key_gain = split_gains(gain_all, model_width)
    segment, position = arrange(seq_lens[0], token_budget)
    live_rows = (segment < SLOTS).astype(jnp.float32)[:, None]
    cosine_lookup, sine_lookup = rope_tables(position)
    pick_mine = pick_core(me, device_count, rows, core)
    pick_mate = pick_core(me, device_count, rows, 1 - core)
    picks = [pick_order(me, device_count, rows, order) for order in orders]

    def both(values):
        return jnp.concatenate([values, swap(values, device_count, 0)], axis=0)

    def both_halves(values):
        mine = exact(values, pick_mine)
        other = swap(exact(values, pick_mate), device_count, 0)
        return jnp.concatenate([mine, other], axis=0)

    stream = tokens.astype(jnp.float32)
    unit_in, scale_in = normalize(stream)
    rescaled_input = (unit_in * attn_gain).astype(jnp.bfloat16)
    qkv = apply_projection(rescaled_input, qkv_w)
    query_unrotated = qkv[:, :qw].reshape(token_budget, QUERY_HEADS, HEAD_WIDTH)
    key_unrotated = qkv[:, qw : qw + kw].reshape(token_budget, VALUE_HEADS, HEAD_WIDTH)
    value_reduced = (
        qkv[:, qw + kw :].astype(jnp.bfloat16).reshape(token_budget, VALUE_HEADS, HEAD_WIDTH)
    )
    query_unit, query_scale = normalize(query_unrotated)
    key_unit, key_scale = normalize(key_unrotated)
    query_rotated = apply_rotary(query_unit * query_norm_weight, cosine_lookup, sine_lookup).astype(
        jnp.bfloat16
    )
    query_rotated = query_rotated.reshape(token_budget, VALUE_HEADS, query_group_width, HEAD_WIDTH)
    key_rot = apply_rotary(key_unit * key_gain, cosine_lookup, sine_lookup).astype(jnp.bfloat16)
    scores = block_scores(query_rotated, key_rot, segment, segment, 0)
    row_top = jnp.max(scores, axis=-1, keepdims=True)
    lifted = jnp.exp(scores - row_top)
    row_mass = jnp.sum(lifted, axis=-1, keepdims=True)
    prob_rows = lifted / row_mass
    prob_low = prob_rows.astype(jnp.bfloat16)
    mixed = jnp.einsum(
        "kgql,lkd->qkgd", prob_low, value_reduced, preferred_element_type=jnp.float32
    )
    attended = mixed.reshape(rows_per_block, QUERY_HEADS * HEAD_WIDTH).astype(jnp.bfloat16)
    branch = back_project(attended, out_wt)
    middle = stream + live_rows * branch
    unit_mid, scale_mid = normalize(middle)
    normed_mid = (unit_mid * ffn_gain).astype(jnp.bfloat16)
    gate_up = apply_projection(normed_mid, gate_up_w)
    gate_pre = gate_up[:, :ff]
    up_pre = gate_up[:, ff:]
    gate_sig = jax.nn.sigmoid(gate_pre)
    gate_act = gate_pre * gate_sig
    hidden = (gate_act * up_pre).astype(jnp.bfloat16)
    grad_out = cotangent.astype(jnp.float32)
    grad_ffn = (live_rows * grad_out).astype(jnp.bfloat16)

    grad_hidden = apply_projection(grad_ffn, down_wt)
    grad_up_pre = (grad_hidden * gate_act).astype(jnp.bfloat16)
    grad_gate_pre = (grad_hidden * up_pre * gate_sig * (1.0 + gate_pre * (1.0 - gate_sig))).astype(
        jnp.bfloat16
    )
    left_mid = both_halves(normed_mid)
    left_ffn = both_halves(grad_ffn)
    owned_down = sum_to_owner(exact(left_ffn, picks[2]), both(hidden), device_count, orders[2])
    owned_gate = sum_to_owner(exact(left_mid, picks[0]), both(grad_gate_pre), device_count, orders[0])
    owned_up = sum_to_owner(exact(left_mid, picks[1]), both(grad_up_pre), device_count, orders[1])

    result = middle + live_rows * back_project(hidden, down_wt)
    grad_mid_norm = back_project(grad_gate_pre, gate_up_w[:, :ff]) + back_project(
        grad_up_pre, gate_up_w[:, ff:]
    )
    grad_ffn_gain = jnp.sum(grad_mid_norm * unit_mid, axis=0)
    grad_middle = grad_out + norm_back(grad_mid_norm * ffn_gain, unit_mid, scale_mid)
    grad_branch = (live_rows * grad_middle).astype(jnp.bfloat16)
    gradient_mixed_values = apply_projection(grad_branch, out_wt).astype(jnp.bfloat16)
    left_branch = both_halves(grad_branch)
    owned_output = sum_to_owner(exact(left_branch, picks[2]), both(attended), device_count, orders[2])
    row_gradient = gradient_mixed_values.reshape(
        rows_per_block, VALUE_HEADS, query_group_width, HEAD_WIDTH
    )
    grad_probs = jnp.einsum(
        "qkgd,lkd->kgql", row_gradient, value_reduced, preferred_element_type=jnp.float32
    )
    centre = jnp.sum(prob_rows * grad_probs, axis=-1, keepdims=True)
    grad_raw = (prob_rows * (grad_probs - centre) * HEAD_WIDTH ** (-0.5)).astype(jnp.bfloat16)
    query_grads = jnp.einsum(
        "kgql,lkd->qkgd", grad_raw, key_rot, preferred_element_type=jnp.float32
    )
    grad_keys = jnp.einsum(
        "kgql,qkgd->lkd", grad_raw, query_rotated, preferred_element_type=jnp.float32
    )
    value_gradient = jnp.einsum(
        "kgql,qkgd->lkd", prob_low, row_gradient, preferred_element_type=jnp.float32
    )
    grad_qrot = query_grads.reshape(token_budget, QUERY_HEADS, HEAD_WIDTH)
    grad_qhead = rotate_back(grad_qrot, cosine_lookup, sine_lookup)
    grad_query_gain = jnp.sum(grad_qhead * query_unit, axis=(0, 1))
    grad_qraw = (
        norm_back(grad_qhead * query_norm_weight, query_unit, query_scale)
        .reshape(token_budget, QUERY_HEADS * HEAD_WIDTH)
        .astype(jnp.bfloat16)
    )
    grad_khead = rotate_back(grad_keys, cosine_lookup, sine_lookup)
    grad_key_gain = jnp.sum(grad_khead * key_unit, axis=(0, 1))
    grad_kraw = (
        norm_back(grad_khead * key_gain, key_unit, key_scale)
        .reshape(token_budget, VALUE_HEADS * HEAD_WIDTH)
        .astype(jnp.bfloat16)
    )
    value_raw_gradient = value_gradient.reshape(token_budget, VALUE_HEADS * HEAD_WIDTH).astype(
        jnp.bfloat16
    )
    left_in = both_halves(rescaled_input)
    owned_query = sum_to_owner(exact(left_in, picks[0]), both(grad_qraw), device_count, orders[0])
    grad_kv = jnp.concatenate([grad_kraw, value_raw_gradient], axis=1)
    owned_kv = sum_to_owner(exact(left_in, picks[1]), both(grad_kv), device_count, orders[1])
    grad_in_norm = back_project(grad_qraw, qkv_w[:, :qw]) + back_project(grad_kv, qkv_w[:, qw:])
    grad_attn_gain = jnp.sum(grad_in_norm * unit_in, axis=0)
    grad_input = grad_middle + norm_back(grad_in_norm * attn_gain, unit_in, scale_in)
    gain_sum = jnp.concatenate(
        [grad_attn_gain, grad_ffn_gain, grad_query_gain, grad_key_gain], axis=0
    ).reshape(device_count, own_gains)
    gain_sum = gain_sum[jnp.arange(device_count, dtype=jnp.int32) ^ me]
    half = device_count
    while half > 1:
        half //= 2
        arrived = swap(gain_sum[half:], device_count, half.bit_length() - 1)
        gain_sum = gain_sum[:half] + arrived
    return (
        result.astype(jnp.bfloat16),
        grad_input,
        owned_query,
        owned_kv[:, :kw],
        owned_kv[:, kw:],
        owned_output.T,
        owned_gate,
        owned_up,
        owned_down.T,
        gain_sum[0],
    )


def solution(mesh):
    in_specs = (
        P("fsdp", None),
        P("fsdp", None),
        P("fsdp", None),
        P("fsdp", None),
        P(None, "fsdp"),
        P("fsdp", None),
        P("fsdp", None),
        P(None, "fsdp"),
        P("fsdp"),
        P("fsdp", None),
        P("fsdp", None),
    )
    out_specs = (
        P("fsdp", None),
        P("fsdp", None),
        P("fsdp", None),
        P("fsdp", None),
        P("fsdp", None),
        P(None, "fsdp"),
        P("fsdp", None),
        P("fsdp", None),
        P(None, "fsdp"),
        P("fsdp"),
    )
    return jax.shard_map(functools.partial(local, mesh.shape["fsdp"]), mesh=mesh, in_specs=in_specs, out_specs=out_specs, check_vma=False)
```

```python
import functools

import jax
import jax.numpy as jnp
from jax import lax
from jax.sharding import PartitionSpec as P

QUERY_HEADS = 16
VALUE_HEADS = 8
HEAD_WIDTH = 128
SLOTS = 4


EPSILON = 1e-06
ROPE_BASE = 1000000.0
MASKED_SCORE = -1e30


def arrange(lengths, token_budget):
    seq_ends = jnp.cumsum(lengths)
    seq_starts = seq_ends - lengths
    places = jnp.arange(token_budget, dtype=jnp.int32)
    segment = jnp.sum((places[:, None] >= seq_ends[None, :]).astype(jnp.int32), axis=1)
    owned_by = segment[:, None] == jnp.arange(SLOTS, dtype=jnp.int32)[None, :]
    first_place = jnp.sum(jnp.where(owned_by, seq_starts[None, :], 0), axis=1)
    return (segment, places - first_place)


def rope_tables(position):
    half_width = HEAD_WIDTH // 2
    inverse = ROPE_BASE ** (-(jnp.arange(half_width, dtype=jnp.float32) * 2.0 / HEAD_WIDTH))
    angles = position.astype(jnp.float32)[:, None] * inverse[None, :]
    angles = jnp.concatenate([angles, angles], axis=-1)
    return (jnp.cos(angles)[:, None, :], jnp.sin(angles)[:, None, :])


def apply_rotary(values, cosine_lookup, sine_lookup):
    half_width = values.shape[-1] // 2
    turned = jnp.concatenate([-values[..., half_width:], values[..., :half_width]], axis=-1)
    return values * cosine_lookup + turned * sine_lookup


def rotate_back(grads, cosine_lookup, sine_lookup):
    half_width = grads.shape[-1] // 2
    turned = grads * sine_lookup
    return grads * cosine_lookup + jnp.concatenate(
        [turned[..., half_width:], -turned[..., :half_width]], axis=-1
    )


def normalize(values):
    row_scale = lax.rsqrt(jnp.mean(values * values, axis=-1, keepdims=True) + EPSILON)
    return (values * row_scale, row_scale)


def norm_back(grads, unit_vals, row_scale):
    return row_scale * (grads - unit_vals * jnp.mean(grads * unit_vals, axis=-1, keepdims=True))


def apply_projection(left, weight):
    return jnp.dot(left, weight, preferred_element_type=jnp.float32)


def back_project(grads, weight):
    return jnp.einsum("tj,ij->ti", grads, weight, preferred_element_type=jnp.float32)


def contract(left, right):
    return jnp.einsum("ti,tj->ij", left, right, preferred_element_type=jnp.float32)


def split_gains(gain_all, model_width):
    gain_all = gain_all.astype(jnp.float32)
    return (
        gain_all[:model_width],
        gain_all[model_width : 2 * model_width],
        gain_all[2 * model_width : 2 * model_width + HEAD_WIDTH],
        gain_all[2 * model_width + HEAD_WIDTH :],
    )


def block_scores(query_block, key_block, seg_rows, seg_keys, first_row):
    row_count = query_block.shape[0]
    key_count = key_block.shape[0]
    raw = jnp.einsum("qkgd,lkd->kgql", query_block, key_block, preferred_element_type=jnp.float32)
    row_at = first_row + jnp.arange(row_count, dtype=jnp.int32)
    key_at = jnp.arange(key_count, dtype=jnp.int32)
    allowed = (seg_rows[:, None] == seg_keys[None, :]) & (row_at[:, None] >= key_at[None, :])
    return jnp.where(allowed[None, None], raw * HEAD_WIDTH ** (-0.5), MASKED_SCORE)


def part_orders(device_count):
    bits = device_count.bit_length() - 1
    if bits == 5:
        return [[1, 2, 3, 4], [2, 1, 3, 4], [3, 1, 2, 4]]
    chip = list(range(1, bits))
    third = (bits - 1) // 3
    return [chip, chip[third:] + chip[:third], chip[2 * third :] + chip[: 2 * third]]


def partners(device_count, bit):
    return [(i, i ^ (1 << bit)) for i in range(device_count)]


def pick_core(me, device_count, rows, core):
    model = device_count * rows
    source = jnp.arange(model, dtype=jnp.int32)[:, None]
    target = jnp.arange(model // 2, dtype=jnp.int32)[None, :]
    wanted = ((target // rows) * 2 + core) * rows + target % rows
    return (source == wanted).astype(jnp.bfloat16)


def pick_order(me, device_count, rows, order):
    half = device_count * rows // 2
    source = jnp.arange(half, dtype=jnp.int32)[:, None]
    target = jnp.arange(half, dtype=jnp.int32)[None, :]
    far = target // rows
    chip = jnp.zeros_like(far)
    last = len(order) - 1
    for place, bit in enumerate(order):
        chip = chip + (((far >> (last - place)) & 1) << (bit - 1))
    wanted = (chip ^ (me // 2)) * rows + target % rows
    return (source == wanted).astype(jnp.bfloat16)


def exact(left, onehot):
    return jnp.dot(left, onehot, preferred_element_type=jnp.float32).astype(jnp.bfloat16)


def swap(values, device_count, bit):
    return lax.ppermute(values, "fsdp", partners(device_count, bit))


class OwnerSum:
    def __init__(self, left, right, device_count, order):
        self.device_count, self.order = device_count, order
        half = left.shape[1] // 2
        sent = contract(left[:, half:], right).astype(jnp.bfloat16)
        self.arrived = swap(sent, device_count, order[0])
        self.kept = contract(left[:, :half], right)
        self.step = 1

    def advance(self):
        if self.arrived is None:
            return
        total = self.kept + self.arrived.astype(jnp.float32)
        if self.step == len(self.order):
            self.kept, self.arrived = total, None
            return
        half = total.shape[0] // 2
        self.arrived = swap(
            total[half:].astype(jnp.bfloat16), self.device_count, self.order[self.step]
        )
        self.kept = total[:half]
        self.step += 1

    def finish(self):
        while self.arrived is not None:
            self.advance()
        return self.kept


def after(values, sums):
    going = [one for one in sums if one.arrived is not None]
    values, landed = lax.optimization_barrier((values, [one.arrived for one in going]))
    for one, arrived in zip(going, landed):
        one.arrived = arrived
        one.advance()
    return values


def local(
    device_count,
    tokens, w_query, w_key, w_value, w_output, w_gate, w_up, w_down, norm_gains, seq_lens, cotangent
):
    me = lax.axis_index("fsdp")
    core = me % 2
    orders = part_orders(device_count)
    token_budget = tokens.shape[0]
    model_width = tokens.shape[1]
    rows = w_query.shape[0]
    qw = w_query.shape[1]
    kw = w_key.shape[1]
    ff = w_gate.shape[1]
    own_gains = norm_gains.shape[0]
    gain_block = jnp.pad(norm_gains[None, :], ((0, rows - 1), (0, 128 - own_gains)))
    gathered = lax.all_gather(
        jnp.concatenate(
            [w_query, w_key, w_value, w_output.T, w_gate, w_up, w_down.T, gain_block], axis=1
        ),
        "fsdp",
        axis=0,
        tiled=True,
    )
    at = qw + 2 * kw
    qkv_w = gathered[:, :at]
    out_wt = gathered[:, at : at + qw]
    at = at + qw
    gate_up_w = gathered[:, at : at + 2 * ff]
    at = at + 2 * ff
    down_wt = gathered[:, at : at + ff]
    at = at + ff
    gain_all = gathered[:, at:].reshape(device_count, rows, 128)[:, 0, :own_gains].reshape(-1)

    query_group_width = QUERY_HEADS // VALUE_HEADS
    rows_per_block = token_budget
    attn_gain, ffn_gain, query_norm_weight, key_gain = split_gains(gain_all, model_width)
    segment, position = arrange(seq_lens[0], token_budget)
    live_rows = (segment < SLOTS).astype(jnp.float32)[:, None]
    cosine_lookup, sine_lookup = rope_tables(position)
    pick_mine = pick_core(me, device_count, rows, core)
    pick_mate = pick_core(me, device_count, rows, 1 - core)
    picks = [pick_order(me, device_count, rows, order) for order in orders]

    def both(values):
        return jnp.concatenate([values, swap(values, device_count, 0)], axis=0)

    def both_halves(values):
        mine = exact(values, pick_mine)
        other = swap(exact(values, pick_mate), device_count, 0)
        return jnp.concatenate([mine, other], axis=0)

    stream = tokens.astype(jnp.float32)
    unit_in, scale_in = normalize(stream)
    rescaled_input = (unit_in * attn_gain).astype(jnp.bfloat16)
    qkv = apply_projection(rescaled_input, qkv_w)
    query_unrotated = qkv[:, :qw].reshape(token_budget, QUERY_HEADS, HEAD_WIDTH)
    key_unrotated = qkv[:, qw : qw + kw].reshape(token_budget, VALUE_HEADS, HEAD_WIDTH)
    value_reduced = (
        qkv[:, qw + kw :].astype(jnp.bfloat16).reshape(token_budget, VALUE_HEADS, HEAD_WIDTH)
    )
    query_unit, query_scale = normalize(query_unrotated)
    key_unit, key_scale = normalize(key_unrotated)
    query_rotated = apply_rotary(query_unit * query_norm_weight, cosine_lookup, sine_lookup).astype(
        jnp.bfloat16
    )
    query_rotated = query_rotated.reshape(token_budget, VALUE_HEADS, query_group_width, HEAD_WIDTH)
    key_rot = apply_rotary(key_unit * key_gain, cosine_lookup, sine_lookup).astype(jnp.bfloat16)
    scores = block_scores(query_rotated, key_rot, segment, segment, 0)
    row_top = jnp.max(scores, axis=-1, keepdims=True)
    lifted = jnp.exp(scores - row_top)
    row_mass = jnp.sum(lifted, axis=-1, keepdims=True)
    prob_rows = lifted / row_mass
    prob_low = prob_rows.astype(jnp.bfloat16)
    mixed = jnp.einsum(
        "kgql,lkd->qkgd", prob_low, value_reduced, preferred_element_type=jnp.float32
    )
    attended = mixed.reshape(rows_per_block, QUERY_HEADS * HEAD_WIDTH).astype(jnp.bfloat16)
    branch = back_project(attended, out_wt)
    middle = stream + live_rows * branch
    unit_mid, scale_mid = normalize(middle)
    normed_mid = (unit_mid * ffn_gain).astype(jnp.bfloat16)
    gate_up = apply_projection(normed_mid, gate_up_w)
    gate_pre = gate_up[:, :ff]
    up_pre = gate_up[:, ff:]
    gate_sig = jax.nn.sigmoid(gate_pre)
    gate_act = gate_pre * gate_sig
    hidden = (gate_act * up_pre).astype(jnp.bfloat16)
    grad_out = cotangent.astype(jnp.float32)
    grad_ffn = (live_rows * grad_out).astype(jnp.bfloat16)

    grad_hidden = apply_projection(grad_ffn, down_wt)
    grad_up_pre = (grad_hidden * gate_act).astype(jnp.bfloat16)
    grad_gate_pre = (grad_hidden * up_pre * gate_sig * (1.0 + gate_pre * (1.0 - gate_sig))).astype(
        jnp.bfloat16
    )
    left_mid = both_halves(normed_mid)
    left_ffn = both_halves(grad_ffn)
    exchanged = (left_mid, left_ffn, both(hidden), both(grad_gate_pre), both(grad_up_pre))

    result = middle + live_rows * back_project(hidden, down_wt)
    grad_mid_norm = back_project(grad_gate_pre, gate_up_w[:, :ff]) + back_project(
        grad_up_pre, gate_up_w[:, ff:]
    )
    (grad_mid_norm, result), exchanged = lax.optimization_barrier(
        ((grad_mid_norm, result), exchanged)
    )
    left_mid, left_ffn, both_hidden, both_gate, both_up = exchanged
    sums = [
        OwnerSum(exact(left_mid, picks[0]), both_gate, device_count, orders[0]),
        OwnerSum(exact(left_mid, picks[1]), both_up, device_count, orders[1]),
        OwnerSum(exact(left_ffn, picks[2]), both_hidden, device_count, orders[2]),
    ]
    grad_ffn_gain = jnp.sum(grad_mid_norm * unit_mid, axis=0)
    grad_middle = grad_out + norm_back(grad_mid_norm * ffn_gain, unit_mid, scale_mid)
    grad_branch = (live_rows * grad_middle).astype(jnp.bfloat16)
    gradient_mixed_values = apply_projection(grad_branch, out_wt).astype(jnp.bfloat16)
    left_branch = both_halves(grad_branch)
    both_attended = both(attended)
    left_in = both_halves(rescaled_input)
    row_gradient = gradient_mixed_values.reshape(
        rows_per_block, VALUE_HEADS, query_group_width, HEAD_WIDTH
    )
    grad_probs = jnp.einsum(
        "qkgd,lkd->kgql", row_gradient, value_reduced, preferred_element_type=jnp.float32
    )
    centre = jnp.sum(prob_rows * grad_probs, axis=-1, keepdims=True)
    grad_raw = (prob_rows * (grad_probs - centre) * HEAD_WIDTH ** (-0.5)).astype(jnp.bfloat16)
    grad_raw, left_branch, both_attended, left_in = after(
        (grad_raw, left_branch, both_attended, left_in), sums
    )
    sums.append(OwnerSum(exact(left_branch, picks[2]), both_attended, device_count, orders[2]))
    query_grads = jnp.einsum(
        "kgql,lkd->qkgd", grad_raw, key_rot, preferred_element_type=jnp.float32
    )
    grad_keys = jnp.einsum(
        "kgql,qkgd->lkd", grad_raw, query_rotated, preferred_element_type=jnp.float32
    )
    value_gradient = jnp.einsum(
        "kgql,qkgd->lkd", prob_low, row_gradient, preferred_element_type=jnp.float32
    )
    query_grads, grad_keys, value_gradient = after((query_grads, grad_keys, value_gradient), sums)
    grad_khead = rotate_back(grad_keys, cosine_lookup, sine_lookup)
    grad_key_gain = jnp.sum(grad_khead * key_unit, axis=(0, 1))
    grad_kraw = (
        norm_back(grad_khead * key_gain, key_unit, key_scale)
        .reshape(token_budget, VALUE_HEADS * HEAD_WIDTH)
        .astype(jnp.bfloat16)
    )
    value_raw_gradient = value_gradient.reshape(token_budget, VALUE_HEADS * HEAD_WIDTH).astype(
        jnp.bfloat16
    )
    grad_kv = jnp.concatenate([grad_kraw, value_raw_gradient], axis=1)
    both_kv = both(grad_kv)
    grad_qrot = query_grads.reshape(token_budget, QUERY_HEADS, HEAD_WIDTH)
    grad_qhead = rotate_back(grad_qrot, cosine_lookup, sine_lookup)
    grad_query_gain = jnp.sum(grad_qhead * query_unit, axis=(0, 1))
    grad_qraw = (
        norm_back(grad_qhead * query_norm_weight, query_unit, query_scale)
        .reshape(token_budget, QUERY_HEADS * HEAD_WIDTH)
        .astype(jnp.bfloat16)
    )
    grad_qraw, both_kv = after((grad_qraw, both_kv), sums)
    sums.append(OwnerSum(exact(left_in, picks[1]), both_kv, device_count, orders[1]))
    both_query = both(grad_qraw)
    grad_in_kv = back_project(grad_kv, qkv_w[:, qw:])
    both_query, grad_in_kv = lax.optimization_barrier((both_query, grad_in_kv))
    sums.append(OwnerSum(exact(left_in, picks[0]), both_query, device_count, orders[0]))
    grad_in_norm = back_project(grad_qraw, qkv_w[:, :qw]) + grad_in_kv
    grad_attn_gain = jnp.sum(grad_in_norm * unit_in, axis=0)
    grad_input = grad_middle + norm_back(grad_in_norm * attn_gain, unit_in, scale_in)
    owned_gate, owned_up, owned_down, owned_output, owned_kv, owned_query = [
        one.finish() for one in sums
    ]
    gain_sum = jnp.concatenate(
        [grad_attn_gain, grad_ffn_gain, grad_query_gain, grad_key_gain], axis=0
    ).reshape(device_count, own_gains)
    gain_sum = gain_sum[jnp.arange(device_count, dtype=jnp.int32) ^ me]
    half = device_count
    while half > 1:
        half //= 2
        arrived = swap(gain_sum[half:], device_count, half.bit_length() - 1)
        gain_sum = gain_sum[:half] + arrived
    return (
        result.astype(jnp.bfloat16),
        grad_input,
        owned_query,
        owned_kv[:, :kw],
        owned_kv[:, kw:],
        owned_output.T,
        owned_gate,
        owned_up,
        owned_down.T,
        gain_sum[0],
    )


def solution(mesh):
    in_specs = (
        P("fsdp", None),
        P("fsdp", None),
        P("fsdp", None),
        P("fsdp", None),
        P(None, "fsdp"),
        P("fsdp", None),
        P("fsdp", None),
        P(None, "fsdp"),
        P("fsdp"),
        P("fsdp", None),
        P("fsdp", None),
    )
    out_specs = (
        P("fsdp", None),
        P("fsdp", None),
        P("fsdp", None),
        P("fsdp", None),
        P("fsdp", None),
        P(None, "fsdp"),
        P("fsdp", None),
        P("fsdp", None),
        P(None, "fsdp"),
        P("fsdp"),
    )
    return jax.shard_map(functools.partial(local, mesh.shape["fsdp"]), mesh=mesh, in_specs=in_specs, out_specs=out_specs, check_vma=False)
```

```python
import functools

import jax
import jax.numpy as jnp
from jax import lax
from jax.sharding import PartitionSpec as P

QUERY_HEADS = 16
VALUE_HEADS = 8
HEAD_WIDTH = 128
SLOTS = 4


EPSILON = 1e-06
ROPE_BASE = 1000000.0
MASKED_SCORE = -1e30


def arrange(lengths, token_budget):
    seq_ends = jnp.cumsum(lengths)
    seq_starts = seq_ends - lengths
    places = jnp.arange(token_budget, dtype=jnp.int32)
    segment = jnp.sum((places[:, None] >= seq_ends[None, :]).astype(jnp.int32), axis=1)
    owned_by = segment[:, None] == jnp.arange(SLOTS, dtype=jnp.int32)[None, :]
    first_place = jnp.sum(jnp.where(owned_by, seq_starts[None, :], 0), axis=1)
    return (segment, places - first_place)


def rope_tables(position):
    half_width = HEAD_WIDTH // 2
    inverse = ROPE_BASE ** (-(jnp.arange(half_width, dtype=jnp.float32) * 2.0 / HEAD_WIDTH))
    angles = position.astype(jnp.float32)[:, None] * inverse[None, :]
    angles = jnp.concatenate([angles, angles], axis=-1)
    return (jnp.cos(angles)[None], jnp.sin(angles)[None])


def turning(dtype=jnp.float32):
    half_width = HEAD_WIDTH // 2
    source = jnp.arange(HEAD_WIDTH, dtype=jnp.int32)[:, None]
    target = jnp.arange(HEAD_WIDTH, dtype=jnp.int32)[None, :]
    plus = (source == target - half_width).astype(dtype)
    return plus - (source == target + half_width).astype(dtype)


def turn(values, matrix):
    return jnp.einsum(
        "htd,de->hte",
        values,
        matrix,
        precision=lax.Precision.HIGHEST,
        preferred_element_type=jnp.float32,
    )


def apply_rotary(values, cosine_lookup, sine_lookup):
    return values * cosine_lookup + turn(values, turning()) * sine_lookup


def rotate_back(grads, cosine_lookup, sine_lookup):
    return grads * cosine_lookup + turn(grads * sine_lookup, turning().T)


def heads_first(values):
    return values.reshape(values.shape[0], -1, HEAD_WIDTH).transpose(1, 0, 2)


def heads_last(values):
    return values.transpose(1, 0, 2).reshape(values.shape[1], -1)


def normalize(values):
    row_scale = lax.rsqrt(jnp.mean(values * values, axis=-1, keepdims=True) + EPSILON)
    return (values * row_scale, row_scale)


def norm_back(grads, unit_vals, row_scale):
    return row_scale * (grads - unit_vals * jnp.mean(grads * unit_vals, axis=-1, keepdims=True))


def apply_projection(left, weight):
    return jnp.dot(left, weight, preferred_element_type=jnp.float32)


def back_project(grads, weight):
    return jnp.einsum("tj,ij->ti", grads, weight, preferred_element_type=jnp.float32)


def contract(left, right):
    return jnp.einsum("ti,tj->ij", left, right, preferred_element_type=jnp.float32)


def split_gains(gain_all, model_width):
    gain_all = gain_all.astype(jnp.float32)
    return (
        gain_all[:model_width],
        gain_all[model_width : 2 * model_width],
        gain_all[2 * model_width : 2 * model_width + HEAD_WIDTH],
        gain_all[2 * model_width + HEAD_WIDTH :],
    )


def block_scores(query_block, key_block, seg_rows, seg_keys, first_row):
    row_count = query_block.shape[2]
    key_count = key_block.shape[1]
    raw = jnp.einsum("kgqd,kld->kgql", query_block, key_block, preferred_element_type=jnp.float32)
    row_at = first_row + jnp.arange(row_count, dtype=jnp.int32)
    key_at = jnp.arange(key_count, dtype=jnp.int32)
    allowed = (seg_rows[:, None] == seg_keys[None, :]) & (row_at[:, None] >= key_at[None, :])
    return jnp.where(allowed[None, None], raw * HEAD_WIDTH ** (-0.5), MASKED_SCORE)


def part_orders(device_count):
    bits = device_count.bit_length() - 1
    if bits == 5:
        return [[1, 2, 3, 4], [2, 1, 3, 4], [3, 1, 2, 4]]
    chip = list(range(1, bits))
    third = (bits - 1) // 3
    return [chip, chip[third:] + chip[:third], chip[2 * third :] + chip[: 2 * third]]


def partners(device_count, bit):
    return [(i, i ^ (1 << bit)) for i in range(device_count)]


def pick_core(me, device_count, rows, core):
    model = device_count * rows
    source = jnp.arange(model, dtype=jnp.int32)[:, None]
    target = jnp.arange(model // 2, dtype=jnp.int32)[None, :]
    wanted = ((target // rows) * 2 + core) * rows + target % rows
    return (source == wanted).astype(jnp.bfloat16)


def pick_order(me, device_count, rows, order):
    half = device_count * rows // 2
    source = jnp.arange(half, dtype=jnp.int32)[:, None]
    target = jnp.arange(half, dtype=jnp.int32)[None, :]
    far = target // rows
    chip = jnp.zeros_like(far)
    last = len(order) - 1
    for place, bit in enumerate(order):
        chip = chip + (((far >> (last - place)) & 1) << (bit - 1))
    wanted = (chip ^ (me // 2)) * rows + target % rows
    return (source == wanted).astype(jnp.bfloat16)


def exact(left, onehot):
    return jnp.dot(left, onehot, preferred_element_type=jnp.float32).astype(jnp.bfloat16)


def swap(values, device_count, bit):
    return lax.ppermute(values, "fsdp", partners(device_count, bit))


def gather_by_doubling(shard, device_count, me, order):
    held = shard
    done = []
    for bit in order:
        arrived = swap(held, device_count, bit)
        place = sum(1 for other in done if other > bit)
        upper = ((me >> bit) & 1) == 1
        held = jnp.stack(
            [jnp.where(upper, arrived, held), jnp.where(upper, held, arrived)], axis=place
        )
        done.append(bit)
    return held


def finish_mates(held, device_count, me):
    arrived = swap(held, device_count, 0)
    upper = (me & 1) == 1
    held = jnp.stack([jnp.where(upper, arrived, held), jnp.where(upper, held, arrived)], axis=-3)
    return held.reshape(-1, held.shape[-1])


class OwnerSum:
    def __init__(self, left, right, device_count, order):
        self.device_count, self.order = device_count, order
        half = left.shape[1] // 2
        sent = contract(left[:, half:], right).astype(jnp.bfloat16)
        self.arrived = swap(sent, device_count, order[0])
        self.kept = contract(left[:, :half], right)
        self.step = 1

    def advance(self):
        if self.arrived is None:
            return
        total = self.kept + self.arrived.astype(jnp.float32)
        if self.step == len(self.order):
            self.kept, self.arrived = total, None
            return
        half = total.shape[0] // 2
        self.arrived = swap(
            total[half:].astype(jnp.bfloat16), self.device_count, self.order[self.step]
        )
        self.kept = total[:half]
        self.step += 1

    def finish(self):
        while self.arrived is not None:
            self.advance()
        return self.kept


def after(values, sums):
    going = [one for one in sums if one.arrived is not None]
    values, landed = lax.optimization_barrier((values, [one.arrived for one in going]))
    for one, arrived in zip(going, landed):
        one.arrived = arrived
        one.advance()
    return values


def local(
    device_count,
    tokens, w_query, w_key, w_value, w_output, w_gate, w_up, w_down, norm_gains, seq_lens, cotangent
):
    me = lax.axis_index("fsdp")
    core = me % 2
    orders = part_orders(device_count)
    token_budget = tokens.shape[0]
    model_width = tokens.shape[1]
    rows = w_query.shape[0]
    qw = w_query.shape[1]
    kw = w_key.shape[1]
    ff = w_gate.shape[1]
    own_gains = norm_gains.shape[0]
    gain_block = jnp.pad(norm_gains[None, :], ((0, rows - 1), (0, 128 - own_gains)))
    gathered = lax.all_gather(
        jnp.concatenate([w_query, w_key, w_value, w_gate, w_up, gain_block], axis=1),
        "fsdp",
        axis=0,
        tiled=True,
    )
    chip_bits = list(range(device_count.bit_length() - 2, 0, -1))
    out_held = gather_by_doubling(
        w_output.T, device_count, me, chip_bits[:-2] + [chip_bits[-1], chip_bits[-2]]
    )
    down_held = gather_by_doubling(w_down.T, device_count, me, chip_bits)
    gathered, out_held, down_held = lax.optimization_barrier((gathered, out_held, down_held))
    out_wt = finish_mates(out_held, device_count, me)
    down_wt = finish_mates(down_held, device_count, me)
    at = qw + 2 * kw
    qkv_w = gathered[:, :at]
    gate_up_w = gathered[:, at : at + 2 * ff]
    at = at + 2 * ff
    gain_all = gathered[:, at:].reshape(device_count, rows, 128)[:, 0, :own_gains].reshape(-1)

    query_group_width = QUERY_HEADS // VALUE_HEADS
    attn_gain, ffn_gain, query_norm_weight, key_gain = split_gains(gain_all, model_width)
    segment, position = arrange(seq_lens[0], token_budget)
    live_rows = (segment < SLOTS).astype(jnp.float32)[:, None]
    cosine_lookup, sine_lookup = rope_tables(position)
    pick_mine = pick_core(me, device_count, rows, core)
    pick_mate = pick_core(me, device_count, rows, 1 - core)
    picks = [pick_order(me, device_count, rows, order) for order in orders]

    def both(values):
        return jnp.concatenate([values, swap(values, device_count, 0)], axis=0)

    def both_halves(values):
        mine = exact(values, pick_mine)
        other = swap(exact(values, pick_mate), device_count, 0)
        return jnp.concatenate([mine, other], axis=0)

    stream = tokens.astype(jnp.float32)
    unit_in, scale_in = normalize(stream)
    rescaled_input = (unit_in * attn_gain).astype(jnp.bfloat16)
    qkv = apply_projection(rescaled_input, qkv_w)
    query_unrotated = heads_first(qkv[:, :qw])
    key_unrotated = heads_first(qkv[:, qw : qw + kw])
    value_reduced = heads_first(qkv[:, qw + kw :].astype(jnp.bfloat16))
    query_unit, query_scale = normalize(query_unrotated)
    key_unit, key_scale = normalize(key_unrotated)
    query_rotated = apply_rotary(query_unit * query_norm_weight, cosine_lookup, sine_lookup).astype(
        jnp.bfloat16
    )
    query_rotated = query_rotated.reshape(VALUE_HEADS, query_group_width, token_budget, HEAD_WIDTH)
    key_rot = apply_rotary(key_unit * key_gain, cosine_lookup, sine_lookup).astype(jnp.bfloat16)
    scores = block_scores(query_rotated, key_rot, segment, segment, 0)
    row_top = jnp.max(scores, axis=-1, keepdims=True)
    lifted = jnp.exp(scores - row_top)
    row_mass = jnp.sum(lifted, axis=-1, keepdims=True)
    prob_rows = lifted / row_mass
    prob_low = prob_rows.astype(jnp.bfloat16)
    mixed = jnp.einsum(
        "kgql,kld->kgqd", prob_low, value_reduced, preferred_element_type=jnp.float32
    )
    attended = heads_last(mixed.reshape(QUERY_HEADS, token_budget, HEAD_WIDTH).astype(jnp.bfloat16))
    branch = back_project(attended, out_wt)
    middle = stream + live_rows * branch
    unit_mid, scale_mid = normalize(middle)
    normed_mid = (unit_mid * ffn_gain).astype(jnp.bfloat16)
    gate_up = apply_projection(normed_mid, gate_up_w)
    gate_pre = gate_up[:, :ff]
    up_pre = gate_up[:, ff:]
    gate_sig = jax.nn.sigmoid(gate_pre)
    gate_act = gate_pre * gate_sig
    hidden = (gate_act * up_pre).astype(jnp.bfloat16)
    grad_out = cotangent.astype(jnp.float32)
    grad_ffn = (live_rows * grad_out).astype(jnp.bfloat16)

    grad_hidden = apply_projection(grad_ffn, down_wt)
    grad_up_pre = (grad_hidden * gate_act).astype(jnp.bfloat16)
    grad_gate_pre = (grad_hidden * up_pre * gate_sig * (1.0 + gate_pre * (1.0 - gate_sig))).astype(
        jnp.bfloat16
    )
    left_mid = both_halves(normed_mid)
    left_ffn = both_halves(grad_ffn)
    exchanged = (left_mid, left_ffn, both(hidden), both(grad_gate_pre), both(grad_up_pre))

    result = middle + live_rows * back_project(hidden, down_wt)
    grad_mid_norm = back_project(grad_gate_pre, gate_up_w[:, :ff]) + back_project(
        grad_up_pre, gate_up_w[:, ff:]
    )
    (grad_mid_norm, result), exchanged = lax.optimization_barrier(
        ((grad_mid_norm, result), exchanged)
    )
    left_mid, left_ffn, both_hidden, both_gate, both_up = exchanged
    sums = [
        OwnerSum(exact(left_mid, picks[0]), both_gate, device_count, orders[0]),
        OwnerSum(exact(left_mid, picks[1]), both_up, device_count, orders[1]),
        OwnerSum(exact(left_ffn, picks[2]), both_hidden, device_count, orders[2]),
    ]
    grad_ffn_gain = jnp.sum(grad_mid_norm * unit_mid, axis=0)
    grad_middle = grad_out + norm_back(grad_mid_norm * ffn_gain, unit_mid, scale_mid)
    grad_branch = (live_rows * grad_middle).astype(jnp.bfloat16)
    gradient_mixed_values = apply_projection(grad_branch, out_wt).astype(jnp.bfloat16)
    left_branch = both_halves(grad_branch)
    both_attended = both(attended)
    left_in = both_halves(rescaled_input)
    row_gradient = heads_first(gradient_mixed_values).reshape(
        VALUE_HEADS, query_group_width, token_budget, HEAD_WIDTH
    )
    grad_probs = jnp.einsum(
        "kgqd,kld->kgql", row_gradient, value_reduced, preferred_element_type=jnp.float32
    )
    centre = jnp.sum(prob_rows * grad_probs, axis=-1, keepdims=True)
    grad_raw = (prob_rows * (grad_probs - centre) * HEAD_WIDTH ** (-0.5)).astype(jnp.bfloat16)
    grad_raw, left_branch, both_attended, left_in = after(
        (grad_raw, left_branch, both_attended, left_in), sums
    )
    sums.append(OwnerSum(exact(left_branch, picks[2]), both_attended, device_count, orders[2]))
    query_grads = jnp.einsum(
        "kgql,kld->kgqd", grad_raw, key_rot, preferred_element_type=jnp.float32
    )
    grad_keys = jnp.einsum(
        "kgql,kgqd->kld", grad_raw, query_rotated, preferred_element_type=jnp.float32
    )
    value_gradient = jnp.einsum(
        "kgql,kgqd->kld", prob_low, row_gradient, preferred_element_type=jnp.float32
    )
    query_grads, grad_keys, value_gradient = after((query_grads, grad_keys, value_gradient), sums)
    grad_khead = rotate_back(grad_keys, cosine_lookup, sine_lookup)
    grad_key_gain = jnp.sum(grad_khead * key_unit, axis=(0, 1))
    grad_kraw = heads_last(
        norm_back(grad_khead * key_gain, key_unit, key_scale).astype(jnp.bfloat16)
    )
    value_raw_gradient = heads_last(value_gradient.astype(jnp.bfloat16))
    grad_kv = jnp.concatenate([grad_kraw, value_raw_gradient], axis=1)
    both_kv = both(grad_kv)
    grad_qrot = query_grads.reshape(QUERY_HEADS, token_budget, HEAD_WIDTH)
    grad_qhead = rotate_back(grad_qrot, cosine_lookup, sine_lookup)
    grad_query_gain = jnp.sum(grad_qhead * query_unit, axis=(0, 1))
    grad_qraw = heads_last(
        norm_back(grad_qhead * query_norm_weight, query_unit, query_scale).astype(jnp.bfloat16)
    )
    grad_qraw, both_kv = after((grad_qraw, both_kv), sums)
    sums.append(OwnerSum(exact(left_in, picks[1]), both_kv, device_count, orders[1]))
    both_query = both(grad_qraw)
    grad_in_kv = back_project(grad_kv, qkv_w[:, qw:])
    both_query, grad_in_kv = lax.optimization_barrier((both_query, grad_in_kv))
    sums.append(OwnerSum(exact(left_in, picks[0]), both_query, device_count, orders[0]))
    grad_in_norm = back_project(grad_qraw, qkv_w[:, :qw]) + grad_in_kv
    grad_attn_gain = jnp.sum(grad_in_norm * unit_in, axis=0)
    grad_input = grad_middle + norm_back(grad_in_norm * attn_gain, unit_in, scale_in)
    owned_gate, owned_up, owned_down, owned_output, owned_kv, owned_query = [
        one.finish() for one in sums
    ]
    gain_sum = jnp.concatenate(
        [grad_attn_gain, grad_ffn_gain, grad_query_gain, grad_key_gain], axis=0
    ).reshape(device_count, own_gains)
    gain_sum = gain_sum[jnp.arange(device_count, dtype=jnp.int32) ^ me]
    half = device_count
    while half > 1:
        half //= 2
        arrived = swap(gain_sum[half:], device_count, half.bit_length() - 1)
        gain_sum = gain_sum[:half] + arrived
    return (
        result.astype(jnp.bfloat16),
        grad_input,
        owned_query,
        owned_kv[:, :kw],
        owned_kv[:, kw:],
        owned_output.T,
        owned_gate,
        owned_up,
        owned_down.T,
        gain_sum[0],
    )


def solution(mesh):
    in_specs = (
        P("fsdp", None),
        P("fsdp", None),
        P("fsdp", None),
        P("fsdp", None),
        P(None, "fsdp"),
        P("fsdp", None),
        P("fsdp", None),
        P(None, "fsdp"),
        P("fsdp"),
        P("fsdp", None),
        P("fsdp", None),
    )
    out_specs = (
        P("fsdp", None),
        P("fsdp", None),
        P("fsdp", None),
        P("fsdp", None),
        P("fsdp", None),
        P(None, "fsdp"),
        P("fsdp", None),
        P("fsdp", None),
        P(None, "fsdp"),
        P("fsdp"),
    )
    return jax.shard_map(functools.partial(local, mesh.shape["fsdp"]), mesh=mesh, in_specs=in_specs, out_specs=out_specs, check_vma=False)
```
